32 devices in a mesh: head: 8 (over z, y), kdim: 4 (over x, core).
Axes of the slice: x: 2, y: 2, z: 4, core: 2. Of those that a mesh axis runs over, the one named last changes fastest.
Arguments:
- hidden: bfloat16 [3, 1024, 8192], P(None, None, 'kdim'), may hold values from -6 to 6
- joined_weight: bfloat16 [3, 8192, 10240], P(None, 'kdim', 'head'), may hold values from -0.0625 to 0.0625
- src_block: int32 [8], replicated, may hold values from 0 to 7, each once
- group_map: int32 [8], replicated, may hold values from 0 to 7, each once
- q_slot: int32 [64], replicated, may hold values from 0 to 7, as said below
Outputs:
- qkv: float32 [3, 1024, 10240], P(None, 'kdim', 'head')
The draws below stay inside these ranges and needn't reach their ends.
Inputs may be any that keep to these rules, and one draw needn't show every extreme that they name: `q_slot`: for every key head g, the entries g * 8 to g * 8 + 7 are a permutation of 0 to 7.
All inputs are finite; a program needn't handle non-finite values.
Results may differ from the reference program's by a relative error of at most 0.0003.
Values may be sent and summed in bfloat16 or wider, within the bound.
A program may use at most 128 MiB of HBM per device.

```python
import jax
import jax.numpy as jnp

D = 8192
HEAD_DIM = 128
Q_HEADS = 64
KV_HEADS = 8
LAYERS = 3
ROWS = 1024
GROUP = 8
BLOCK = 1280
JOINED = 10240
N_HEAD = 8


def draw_q_slot(key, part):
    group_keys = jax.random.split(jax.random.fold_in(key, 17), KV_HEADS)
    perms = jax.vmap(lambda one_key: jax.random.permutation(one_key, Q_HEADS // KV_HEADS))(group_keys)
    return perms.reshape(-1).astype(jnp.int32)


def block_scale(rng, extent, shards, least, largest):
    loudness, own = 1.0, jax.random.fold_in(rng, 6)
    for position, blocks in shards:
        steps = jnp.exp(jax.random.uniform(jax.random.fold_in(own, position), (blocks,), jnp.float32, least / len(shards), largest / len(shards)))
        loudness = loudness * jnp.repeat(steps, extent[position] // blocks).reshape([-1 if axis == position else 1 for axis in range(len(extent))])
    return loudness


def centred(stream_key, shape, width, bound, cuts=(), kind=jnp.bfloat16):
    values = jax.random.normal(stream_key, shape, jnp.float32) * width
    if len(cuts) > 0:
        values = block_scale(stream_key, shape, cuts, -0.22, 0.18) * values
    return jnp.clip(values, min=-bound, max=bound).astype(kind)


def setup_inputs(seed: int = 0) -> dict:
    seeds = jax.random.split(jax.random.key(seed), 6)
    hidden = centred(seeds[0], (LAYERS, ROWS, D), 1.0, 6.0, ((2, 4),))
    joined_weight = centred(seeds[1], (LAYERS, D, JOINED), D ** -0.5, 0.0625, ((1, 4), (2, 8)))
    src_block = jax.random.permutation(seeds[2], KV_HEADS).astype(jnp.int32)
    group_map = jax.random.permutation(seeds[3], KV_HEADS).astype(jnp.int32)
    q_slot = draw_q_slot(jax.random.fold_in(seeds[5], 71), 0)
    return dict(hidden=hidden, joined_weight=joined_weight, src_block=src_block, group_map=group_map, q_slot=q_slot)


def build_table(src_block, group_map, q_slot):
    group_devs = N_HEAD // KV_HEADS
    slot_count = Q_HEADS // N_HEAD
    devices = jnp.arange(N_HEAD, dtype=jnp.int32)
    group_ids = devices // group_devs
    quarter = devices % group_devs
    rank_ids = jnp.arange(KV_HEADS, dtype=jnp.int32)
    owner = jnp.sum(rank_ids[None, :] * (group_map[None, :] == group_ids[:, None]), axis=1).astype(jnp.int32)
    block_start = (jnp.sum(src_block[None, :] * (rank_ids[None, :] == owner[:, None]), axis=1) * BLOCK).astype(jnp.int32)
    members = (owner[:, None] * GROUP + jnp.arange(GROUP, dtype=jnp.int32)[None, :]).astype(jnp.int32)
    member_slot = q_slot[members]
    positions = quarter[:, None] * slot_count + jnp.arange(slot_count, dtype=jnp.int32)[None, :]
    local_head = jnp.sum(jnp.arange(GROUP, dtype=jnp.int32)[None, None, :] * (member_slot[:, None, :] == positions[:, :, None]), axis=2).astype(jnp.int32)
    q_cols = block_start[:, None, None] + local_head[:, :, None] * HEAD_DIM + jnp.arange(HEAD_DIM, dtype=jnp.int32)[None, None, :]
    kv_cols = block_start[:, None] + GROUP * HEAD_DIM + jnp.arange(2 * HEAD_DIM, dtype=jnp.int32)[None, :]
    columns = jnp.concatenate([q_cols.reshape(N_HEAD, slot_count * HEAD_DIM), kv_cols], axis=1)
    return columns.reshape(-1).astype(jnp.int32)


def reference(hidden, joined_weight, src_block, group_map, q_slot):
    columns = build_table(src_block, group_map, q_slot)
    results = []
    for layer in range(LAYERS):
        full = jnp.dot(hidden[layer], joined_weight[layer], preferred_element_type=jnp.float32)
        results.append(full[:, columns])
    return jnp.stack(results, axis=0)
```

```python
import jax
import jax.numpy as jnp
from jax import lax
from jax.sharding import PartitionSpec as P

HEAD_DIM = 128
Q_HEADS = 64
KV_HEADS = 8
GROUP = 8


def from_partner(block, axis, stride):
    count = lax.axis_size(axis)
    route = []
    for low in range(count):
        high = low | 1 << stride
        if high != low and high < count:
            route += [(low, high), (high, low)]
    return lax.ppermute(block, axis, route)


def lookup(table, where_at):
    entries = jnp.arange(table.shape[0], dtype=jnp.int32)
    return jnp.sum(table[None, :] * (entries[None, :] == where_at[:, None]), axis=1)


def regroup(
    payload,
    start_keys,
    position,
    quarter,
    head_index,
    group_slots,
    slot_count,
    low_bits,
    sort_bits,
    pair_swap,
    part_swap,
):
    places = jnp.arange(KV_HEADS, dtype=jnp.int32)
    key_list = start_keys
    for level in range(1, sort_bits + 1):
        for stride in reversed(range(level)):
            partner = pair_swap(payload, low_bits + stride)
            partner_places = jnp.bitwise_xor(places, 1 << stride)
            partner_keys = lookup(key_list, partner_places)
            upper_half = jnp.bitwise_and(jnp.right_shift(places, stride), 1) == 1
            ascending = jnp.bitwise_and(jnp.right_shift(places, level), 1) == 0
            smaller = key_list < partner_keys
            keep_own = (jnp.logical_not(upper_half) == smaller) == ascending
            keep_mine = jnp.any(jnp.logical_and(keep_own, places == position))
            payload = jnp.where(keep_mine, payload, partner)
            key_list = jnp.where(keep_own, key_list, partner_keys)
    for which_bit in range(low_bits):
        partner = part_swap(payload, which_bit)
        upper_side = jnp.bitwise_and(jnp.right_shift(head_index, which_bit), 1) == 1
        payload = jnp.where(
            upper_side,
            jnp.concatenate([partner, payload], axis=2),
            jnp.concatenate([payload, partner], axis=2),
        )
    pieces = []
    for offset_slot in range(slot_count):
        wanted = quarter * slot_count + offset_slot
        local_head = jnp.sum(jnp.arange(GROUP, dtype=jnp.int32) * (group_slots == wanted))
        pieces.append(lax.dynamic_slice_in_dim(payload, local_head * HEAD_DIM, HEAD_DIM, axis=2))
    pieces.append(payload[:, :, GROUP * HEAD_DIM :])
    return jnp.concatenate(pieces, axis=2)


def regroup_dense(payload, start_keys, group_slots, slot_count):
    heads = lax.axis_size("head")
    depth = payload.shape[1] // heads
    ids = jnp.arange(heads, dtype=jnp.int32)
    source = jnp.sum(ids[None, :] * (start_keys[None, :] == ids[:, None]), axis=1)
    spread = lax.all_to_all(payload, "head", split_axis=1, concat_axis=1, tiled=True)
    picked = jnp.concatenate(
        [lax.dynamic_slice_in_dim(spread, source[d] * depth, depth, axis=1) for d in range(heads)], axis=1
    )
    payload = lax.all_to_all(picked, "head", split_axis=1, concat_axis=1, tiled=True)
    pieces = []
    for wanted in range(slot_count):
        local_head = jnp.sum(jnp.arange(GROUP, dtype=jnp.int32) * (group_slots == wanted))
        pieces.append(lax.dynamic_slice_in_dim(payload, local_head * HEAD_DIM, HEAD_DIM, axis=2))
    pieces.append(payload[:, :, GROUP * HEAD_DIM :])
    return jnp.concatenate(pieces, axis=2)


def on_device(hidden, joined_weight, src_block, group_map, q_slot):
    head_count = lax.axis_size("head")
    per_group = head_count // KV_HEADS
    low_bits = per_group.bit_length() - 1
    sort_bits = KV_HEADS.bit_length() - 1
    slot_count = Q_HEADS // head_count
    head_index = lax.axis_index("head")
    position = head_index // per_group
    quarter = head_index % per_group
    rank_ids = jnp.arange(KV_HEADS, dtype=jnp.int32)
    rank_at = jnp.sum(rank_ids[None, :] * (src_block[None, :] == rank_ids[:, None]), axis=1)
    start_keys = lookup(group_map, rank_at)
    rank_here = jnp.sum(rank_ids * (group_map == position))
    group_slots = lax.dynamic_slice_in_dim(q_slot, rank_here * GROUP, GROUP)
    partial_value = jnp.einsum(
        "lrd,ldc->lrc", hidden, joined_weight, preferred_element_type=jnp.float32
    )
    summed = lax.psum_scatter(partial_value, "kdim", scatter_dimension=1, tiled=True)
    if head_count == KV_HEADS and summed.shape[1] % head_count == 0:
        return regroup_dense(summed, start_keys, group_slots, slot_count)
    return regroup(
        summed,
        start_keys,
        position,
        quarter,
        head_index,
        group_slots,
        slot_count,
        low_bits,
        sort_bits,
        lambda piece, which_bit: from_partner(piece, "head", which_bit),
        lambda piece, which_bit: from_partner(piece, "head", which_bit),
    )


def solution(mesh):
    return jax.shard_map(
        on_device,
        mesh=mesh,
        in_specs=(P(None, None, "kdim"), P(None, "kdim", "head"), P(), P(), P()),
        out_specs=P(None, "kdim", "head"),
        check_vma=False,
    )
```

```python
import jax
import jax.numpy as jnp
from jax import lax
import functools
from jax.experimental import pallas as pl
from jax.experimental.pallas import tpu as pltpu
from jax.sharding import PartitionSpec as P

HEAD_DIM = 128
Q_HEADS = 64
KV_HEADS = 8
GROUP = 8


def from_partner(block, axis, stride):
    count = lax.axis_size(axis)
    route = []
    for low in range(count):
        high = low | 1 << stride
        if high != low and high < count:
            route += [(low, high), (high, low)]
    return lax.ppermute(block, axis, route)


def lookup(table, where_at):
    entries = jnp.arange(table.shape[0], dtype=jnp.int32)
    return jnp.sum(table[None, :] * (entries[None, :] == where_at[:, None]), axis=1)


def regroup(
    payload,
    start_keys,
    position,
    quarter,
    head_index,
    group_slots,
    slot_count,
    low_bits,
    sort_bits,
    pair_swap,
    part_swap,
):
    places = jnp.arange(KV_HEADS, dtype=jnp.int32)
    key_list = start_keys
    for level in range(1, sort_bits + 1):
        for stride in reversed(range(level)):
            partner = pair_swap(payload, low_bits + stride)
            partner_places = jnp.bitwise_xor(places, 1 << stride)
            partner_keys = lookup(key_list, partner_places)
            upper_half = jnp.bitwise_and(jnp.right_shift(places, stride), 1) == 1
            ascending = jnp.bitwise_and(jnp.right_shift(places, level), 1) == 0
            smaller = key_list < partner_keys
            keep_own = (jnp.logical_not(upper_half) == smaller) == ascending
            keep_mine = jnp.any(jnp.logical_and(keep_own, places == position))
            payload = jnp.where(keep_mine, payload, partner)
            key_list = jnp.where(keep_own, key_list, partner_keys)
    for which_bit in range(low_bits):
        partner = part_swap(payload, which_bit)
        upper_side = jnp.bitwise_and(jnp.right_shift(head_index, which_bit), 1) == 1
        payload = jnp.where(
            upper_side,
            jnp.concatenate([partner, payload], axis=2),
            jnp.concatenate([payload, partner], axis=2),
        )
    pieces = []
    for offset_slot in range(slot_count):
        wanted = quarter * slot_count + offset_slot
        local_head = jnp.sum(jnp.arange(GROUP, dtype=jnp.int32) * (group_slots == wanted))
        pieces.append(lax.dynamic_slice_in_dim(payload, local_head * HEAD_DIM, HEAD_DIM, axis=2))
    pieces.append(payload[:, :, GROUP * HEAD_DIM :])
    return jnp.concatenate(pieces, axis=2)


SPLIT = 2
TOP = 32767.0
TINY = 1e-30
CHUNK = 16


def quantum(peak):
    peak = jnp.maximum(peak, TINY)
    return TOP / peak, peak * (1.0 / TOP)


def spread_tile(tile, columns):
    return jnp.concatenate([jnp.concatenate([tile] * (CHUNK // 8), axis=0)] * (columns // 128), axis=1)


def fold_peak(value):
    value = jnp.abs(value)
    peak = value[:, :128]
    for start in range(128, value.shape[1], 128):
        peak = jnp.maximum(peak, value[:, start : start + 128])
    return jnp.maximum(peak[:8], peak[8:])


def code(value, inverse):
    return jnp.round(value * inverse).astype(jnp.int32).astype(jnp.int16)


def decode(coded, scale):
    return coded.astype(jnp.int32).astype(jnp.float32) * scale


def exchange_kernel(
    layers, heads, stages, band, source_ref, hidden_ref, weight_ref, out_ref, scale_ref,
    hbuf, wbuf, core_out, core_in, mine, hold, x_out, x_in, x_scale_out, x_scale_in,
    spread_out, own_scale, bound_out, *rest,
):
    spread_in = rest[:stages]
    load_sem, core_send, core_recv, x_send, x_recv, p_send, p_recv, s_send, s_recv, b_send, b_recv = rest[stages:]
    columns = weight_ref.shape[2]
    quarter = hidden_ref.shape[1] // 4
    me = lax.axis_index("head")
    k = lax.axis_index("kdim")
    core, x = lax.rem(k, 2), lax.div(k, 2)
    core_peer = x * 2 + 1 - core
    x_peer = (1 - x) * 2 + core

    def loads(layer):
        slot = layer % 2
        return (
            pltpu.make_async_copy(hidden_ref.at[layer], hbuf.at[slot], load_sem.at[slot, 0]),
            pltpu.make_async_copy(weight_ref.at[layer], wbuf.at[slot], load_sem.at[slot, 1]),
        )

    for layer in range(min(2, layers)):
        for copy in loads(layer):
            copy.start()

    barrier = pltpu.get_barrier_semaphore()
    for peer in (core_peer, x_peer):
        pl.semaphore_signal(barrier, inc=1, device_id={"kdim": peer}, device_id_type=pl.DeviceIdType.MESH)

    def greet(offset, carry):
        pl.semaphore_signal(
            barrier, inc=1, device_id={"head": lax.rem(me + offset, heads)}, device_id_type=pl.DeviceIdType.MESH
        )
        return carry

    lax.fori_loop(1, heads, greet, 0)
    pl.semaphore_wait(barrier, heads + 1)

    def remote(source, target, send, recv, peer):
        return pltpu.make_async_remote_copy(
            src_ref=source, dst_ref=target, send_sem=send, recv_sem=recv,
            device_id=peer, device_id_type=pl.DeviceIdType.MESH,
        )

    def core_copy(stage):
        return remote(
            core_out.at[stage], core_in.at[stage], core_send.at[stage], core_recv.at[stage], {"kdim": core_peer}
        )

    def x_copies(stage):
        return (
            remote(x_out.at[stage], x_in.at[stage], x_send.at[stage, 0], x_recv.at[stage, 0], {"kdim": x_peer}),
            remote(
                x_scale_out.at[stage], x_scale_in.at[stage], x_send.at[stage, 1], x_recv.at[stage, 1],
                {"kdim": x_peer},
            ),
        )

    def spread_copies(stage, peer, slot):
        return (
            remote(
                spread_out.at[stage, peer], spread_in[stage].at[slot], p_send.at[stage, peer],
                p_recv.at[stage, slot], {"head": peer},
            ),
            remote(
                own_scale.at[stage], scale_ref.at[stage, slot], s_send.at[stage, peer],
                s_recv.at[stage, slot], {"head": peer},
            ),
        )

    def bound_copy(stage, peer, slot):
        return remote(
            bound_out.at[stage, peer], out_ref.at[stage, slot], b_send.at[stage, peer],
            b_recv.at[stage, slot], {"head": peer},
        )

    def own_scale_copy(stage):
        return pltpu.make_async_copy(own_scale.at[stage], scale_ref.at[stage, me], s_recv.at[stage, me])

    def own_bound_copy(stage):
        return pltpu.make_async_copy(bound_out.at[stage, me], out_ref.at[stage, me], b_recv.at[stage, me])

    width = 256
    tiles = columns // width
    chunks = band // CHUNK

    def product(stage, which_core, target):
        slot, start = (stage // SPLIT) % 2, (stage % SPLIT) * band

        def body(step, carry):
            half, tile = lax.div(step, tiles), lax.rem(step, tiles)
            row = pl.multiple_of((half * 2 + which_core) * quarter + start, band)
            column = pl.multiple_of(tile * width, width)
            target[half, :, pl.ds(column, width)] = jnp.dot(
                hbuf[slot, pl.ds(row, band), :], wbuf[slot, :, pl.ds(column, width)],
                preferred_element_type=jnp.float32,
            )
            return carry

        lax.fori_loop(0, 2 * tiles, body, 0)

    def rows_of(chunk):
        return pl.ds(pl.multiple_of(chunk * CHUNK, CHUNK), CHUNK)

    zero_peak = jnp.zeros((8, 128), jnp.float32)

    def multiply(stage):
        if stage % SPLIT == 0:
            for copy in loads(stage // SPLIT):
                copy.wait()
        product(stage, 1 - core, core_out.at[stage])
        core_copy(stage).start()
        product(stage, core, mine)
        layer = stage // SPLIT
        if stage % SPLIT == SPLIT - 1 and layer + 2 < layers:
            for copy in loads(layer + 2):
                copy.start()
        core_copy(stage).wait_recv()

        def add(chunk, peak):
            rows = rows_of(chunk)
            hold[stage, rows, :] = mine[x, rows, :] + core_in[stage, x, rows, :]
            other = mine[1 - x, rows, :] + core_in[stage, 1 - x, rows, :]
            mine[1 - x, rows, :] = other
            return jnp.maximum(peak, fold_peak(other))

        inverse, scale = quantum(lax.fori_loop(0, chunks, add, zero_peak))
        x_scale_out[stage] = scale
        inverse = spread_tile(inverse, columns)

        def pack(chunk, carry):
            rows = rows_of(chunk)
            x_out[stage, rows, :] = code(mine[1 - x, rows, :], inverse)
            return carry

        lax.fori_loop(0, chunks, pack, 0)
        for copy in x_copies(stage):
            copy.start()

    def reduce(stage):
        for copy in x_copies(stage):
            copy.wait_recv()
        arrived = spread_tile(x_scale_in[stage], columns)

        def add(chunk, peak):
            rows = rows_of(chunk)
            total = hold[stage, rows, :] + decode(x_in[stage, rows, :], arrived)
            hold[stage, rows, :] = total
            return jnp.maximum(peak, fold_peak(total))

        inverse, scale = quantum(lax.fori_loop(0, chunks, add, zero_peak))
        own_scale[stage] = scale
        inverse = spread_tile(inverse, columns)
        per = chunks // heads

        def pack(chunk, carry):
            spread_out[stage, lax.div(chunk, per), rows_of(lax.rem(chunk, per)), :] = code(
                hold[stage, rows_of(chunk), :], inverse
            )
            return carry

        lax.fori_loop(0, chunks, pack, 0)

        def send(offset, carry):
            for copy in spread_copies(stage, lax.rem(me + offset, heads), me):
                copy.start()
            return carry

        lax.fori_loop(1, heads, send, 0)
        own_scale_copy(stage).start()
        spread_in[stage][me] = spread_out[stage, me]

    def forward(stage):
        def arrive(offset, carry):
            peer = lax.rem(me + offset, heads)
            spread_copies(stage, peer, peer)[0].wait_recv()
            return carry

        lax.fori_loop(1, heads, arrive, 0)

        def send(offset, carry):
            peer = lax.rem(me + offset, heads)
            bound_out[stage, peer] = spread_in[stage][source_ref[peer]]
            bound_copy(stage, peer, me).start()
            return carry

        lax.fori_loop(1, heads, send, 0)
        bound_out[stage, me] = spread_in[stage][source_ref[me]]
        own_bound_copy(stage).start()

    for step in range(stages + 4):
        if step < stages:
            multiply(step)
        if 0 <= step - 1 < stages:
            reduce(step - 1)
        if 0 <= step - 2 < stages:
            forward(step - 2)

    def finish(stage, carry):
        core_copy(stage).wait_send()
        for copy in x_copies(stage):
            copy.wait_send()

        def one(offset, inner):
            peer = lax.rem(me + offset, heads)
            for copy in (
                remote(
                    spread_out.at[stage, peer], out_ref.at[stage, peer], p_send.at[stage, peer],
                    p_recv.at[stage, peer], {"head": peer},
                ),
                remote(
                    own_scale.at[stage], scale_ref.at[stage, peer], s_send.at[stage, peer],
                    s_recv.at[stage, peer], {"head": peer},
                ),
                bound_copy(stage, peer, peer),
            ):
                copy.wait_send()
            spread_scale = remote(
                own_scale.at[stage], scale_ref.at[stage, peer], s_send.at[stage, peer],
                s_recv.at[stage, peer], {"head": peer},
            )
            spread_scale.wait_recv()
            bound_copy(stage, peer, peer).wait_recv()
            return inner

        lax.fori_loop(1, heads, one, 0)
        own_scale_copy(stage).wait()
        own_bound_copy(stage).wait()
        return carry

    lax.fori_loop(0, stages, finish, 0)


def place_kernel(where_ref, coded_ref, scale_ref, out_ref):
    rows = coded_ref.shape[1]
    scale = jnp.concatenate([scale_ref[0, 0]] * (rows // 8), axis=0)
    for slot in range(GROUP):
        start = pl.multiple_of(where_ref[1 + slot] * HEAD_DIM, HEAD_DIM)
        out_ref[0, :, slot * HEAD_DIM : (slot + 1) * HEAD_DIM] = decode(
            coded_ref[0, :, pl.ds(start, HEAD_DIM)], scale
        )
    for start in range(GROUP * HEAD_DIM, coded_ref.shape[2], HEAD_DIM):
        out_ref[0, :, start : start + HEAD_DIM] = decode(coded_ref[0, :, start : start + HEAD_DIM], scale)


def fused(hidden, joined_weight, start_keys, head_index, group_slots):
    layers, rows, depth = hidden.shape
    columns = joined_weight.shape[2]
    heads = lax.axis_size("head")
    stages = layers * SPLIT
    band = rows // 4 // SPLIT
    piece = band // heads
    ids = jnp.arange(heads, dtype=jnp.int32)
    source = jnp.sum(ids[None, :] * (start_keys[None, :] == ids[:, None]), axis=1).astype(jnp.int32)
    f32, i16 = jnp.float32, jnp.int16
    hbm = pl.BlockSpec(memory_space=pl.ANY)
    dma = pltpu.SemaphoreType.DMA
    coded, scales = pl.pallas_call(
        functools.partial(exchange_kernel, layers, heads, stages, band),
        out_shape=[
            jax.ShapeDtypeStruct((stages, heads, piece, columns), i16),
            jax.ShapeDtypeStruct((stages, heads, 8, 128), f32),
        ],
        in_specs=[pl.BlockSpec(memory_space=pltpu.SMEM), hbm, hbm],
        out_specs=[hbm, hbm],
        scratch_shapes=[
            pltpu.VMEM((2, rows, depth), hidden.dtype),
            pltpu.VMEM((2, depth, columns), joined_weight.dtype),
            pltpu.VMEM((stages, 2, band, columns), f32),
            pltpu.VMEM((stages, 2, band, columns), f32),
            pltpu.VMEM((2, band, columns), f32),
            pltpu.VMEM((stages, band, columns), f32),
            pltpu.VMEM((stages, band, columns), i16),
            pltpu.VMEM((stages, band, columns), i16),
            pltpu.VMEM((stages, 8, 128), f32),
            pltpu.VMEM((stages, 8, 128), f32),
            pltpu.VMEM((stages, heads, piece, columns), i16),
            pltpu.VMEM((stages, 8, 128), f32),
            pltpu.VMEM((stages, heads, piece, columns), i16),
        ]
        + [pltpu.VMEM((heads, piece, columns), i16) for _ in range(stages)]
        + [dma((2, 2)), dma((stages,)), dma((stages,)), dma((stages, 2)), dma((stages, 2))]
        + [dma((stages, heads)) for _ in range(6)],
        compiler_params=pltpu.CompilerParams(
            collective_id=0, has_side_effects=True, vmem_limit_bytes=58 * 2**20
        ),
        cost_estimate=pl.CostEstimate(
            flops=2 * layers * rows * depth * columns, transcendentals=0,
            bytes_accessed=2 * layers * depth * (rows + columns),
        ),
    )(source, hidden, joined_weight)
    slots = jnp.arange(GROUP, dtype=jnp.int32)
    local = jnp.sum(slots[None, :] * (group_slots[None, :] == slots[:, None]), axis=1)
    mine = jnp.sum(source * (ids == head_index))
    where_at = jnp.concatenate([mine[None], local]).astype(jnp.int32)
    out = pl.pallas_call(
        place_kernel,
        grid_spec=pltpu.PrefetchScalarGridSpec(
            num_scalar_prefetch=1,
            grid=(stages,),
            in_specs=[
                pl.BlockSpec((1, band, columns), lambda s, where_ref: (s, 0, 0)),
                pl.BlockSpec((1, 1, 8, 128), lambda s, where_ref: (s, where_ref[0], 0, 0)),
            ],
            out_specs=pl.BlockSpec((1, band, columns), lambda s, where_ref: (s, 0, 0)),
        ),
        out_shape=jax.ShapeDtypeStruct((stages, band, columns), f32),
    )(where_at, coded.reshape(stages, band, columns), scales)
    return out.reshape(layers, rows // 4, columns)


def on_device(hidden, joined_weight, src_block, group_map, q_slot):
    head_count = lax.axis_size("head")
    per_group = head_count // KV_HEADS
    low_bits = per_group.bit_length() - 1
    sort_bits = KV_HEADS.bit_length() - 1
    slot_count = Q_HEADS // head_count
    head_index = lax.axis_index("head")
    position = head_index // per_group
    quarter = head_index % per_group
    rank_ids = jnp.arange(KV_HEADS, dtype=jnp.int32)
    rank_at = jnp.sum(rank_ids[None, :] * (src_block[None, :] == rank_ids[:, None]), axis=1)
    start_keys = lookup(group_map, rank_at)
    rank_here = jnp.sum(rank_ids * (group_map == position))
    group_slots = lax.dynamic_slice_in_dim(q_slot, rank_here * GROUP, GROUP)
    heads_fit = head_count == KV_HEADS and joined_weight.shape[2] == (GROUP + 2) * HEAD_DIM
    if heads_fit and lax.axis_size("kdim") == 4 and hidden.shape[1] % (4 * SPLIT * CHUNK * head_count) == 0:
        return fused(hidden, joined_weight, start_keys, head_index, group_slots)
    partial_value = jnp.einsum(
        "lrd,ldc->lrc", hidden, joined_weight, preferred_element_type=jnp.float32
    )
    summed = lax.psum_scatter(partial_value, "kdim", scatter_dimension=1, tiled=True)
    return regroup(
        summed,
        start_keys,
        position,
        quarter,
        head_index,
        group_slots,
        slot_count,
        low_bits,
        sort_bits,
        lambda piece, which_bit: from_partner(piece, "head", which_bit),
        lambda piece, which_bit: from_partner(piece, "head", which_bit),
    )


def solution(mesh):
    return jax.shard_map(
        on_device,
        mesh=mesh,
        in_specs=(P(None, None, "kdim"), P(None, "kdim", "head"), P(), P(), P()),
        out_specs=P(None, "kdim", "head"),
        check_vma=False,
    )
```

```python
import jax
import jax.numpy as jnp
from jax import lax
import functools
from jax.experimental import pallas as pl
from jax.experimental.pallas import tpu as pltpu
from jax.sharding import PartitionSpec as P

HEAD_DIM = 128
Q_HEADS = 64
KV_HEADS = 8
GROUP = 8


def from_partner(block, axis, stride):
    count = lax.axis_size(axis)
    route = []
    for low in range(count):
        high = low | 1 << stride
        if high != low and high < count:
            route += [(low, high), (high, low)]
    return lax.ppermute(block, axis, route)


def lookup(table, where_at):
    entries = jnp.arange(table.shape[0], dtype=jnp.int32)
    return jnp.sum(table[None, :] * (entries[None, :] == where_at[:, None]), axis=1)


def regroup(
    payload,
    start_keys,
    position,
    quarter,
    head_index,
    group_slots,
    slot_count,
    low_bits,
    sort_bits,
    pair_swap,
    part_swap,
):
    places = jnp.arange(KV_HEADS, dtype=jnp.int32)
    key_list = start_keys
    for level in range(1, sort_bits + 1):
        for stride in reversed(range(level)):
            partner = pair_swap(payload, low_bits + stride)
            partner_places = jnp.bitwise_xor(places, 1 << stride)
            partner_keys = lookup(key_list, partner_places)
            upper_half = jnp.bitwise_and(jnp.right_shift(places, stride), 1) == 1
            ascending = jnp.bitwise_and(jnp.right_shift(places, level), 1) == 0
            smaller = key_list < partner_keys
            keep_own = (jnp.logical_not(upper_half) == smaller) == ascending
            keep_mine = jnp.any(jnp.logical_and(keep_own, places == position))
            payload = jnp.where(keep_mine, payload, partner)
            key_list = jnp.where(keep_own, key_list, partner_keys)
    for which_bit in range(low_bits):
        partner = part_swap(payload, which_bit)
        upper_side = jnp.bitwise_and(jnp.right_shift(head_index, which_bit), 1) == 1
        payload = jnp.where(
            upper_side,
            jnp.concatenate([partner, payload], axis=2),
            jnp.concatenate([payload, partner], axis=2),
        )
    pieces = []
    for offset_slot in range(slot_count):
        wanted = quarter * slot_count + offset_slot
        local_head = jnp.sum(jnp.arange(GROUP, dtype=jnp.int32) * (group_slots == wanted))
        pieces.append(lax.dynamic_slice_in_dim(payload, local_head * HEAD_DIM, HEAD_DIM, axis=2))
    pieces.append(payload[:, :, GROUP * HEAD_DIM :])
    return jnp.concatenate(pieces, axis=2)


SPLIT = 2
TOP = 32767.0
TINY = 1e-30
CHUNK = 16


def quantum(peak):
    peak = jnp.maximum(peak, TINY)
    return TOP / peak, peak * (1.0 / TOP)


def spread_tile(tile, columns):
    return jnp.concatenate([jnp.concatenate([tile] * (CHUNK // 8), axis=0)] * (columns // 128), axis=1)


def fold_peak(value):
    value = jnp.abs(value)
    peak = value[:, :128]
    for start in range(128, value.shape[1], 128):
        peak = jnp.maximum(peak, value[:, start : start + 128])
    return jnp.maximum(peak[:8], peak[8:])


def code(value, inverse):
    return jnp.round(value * inverse).astype(jnp.int32).astype(jnp.int16)


def decode(coded, scale):
    return coded.astype(jnp.int32).astype(jnp.float32) * scale


def exchange_kernel(
    layers, heads, stages, band, source_block_ref, group_map_ref, hidden_ref, weight_ref, out_ref, scale_ref,
    hbuf, wbuf, core_out, core_in, mine, hold, x_out, x_in, x_scale_out, x_scale_in,
    spread_out, own_scale, bound_out, *rest,
):
    spread_in = rest[:stages]
    load_sem, core_send, core_recv, x_send, x_recv, p_send, p_recv, s_send, s_recv, b_send, b_recv = rest[stages:]
    columns = weight_ref.shape[2]
    quarter = hidden_ref.shape[1] // 4
    me = lax.axis_index("head")
    k = lax.axis_index("kdim")
    core, x = lax.rem(k, 2), lax.div(k, 2)
    core_peer = x * 2 + 1 - core
    x_peer = (1 - x) * 2 + core

    def loads(layer):
        slot = layer % 2
        rows = [
            [
                pltpu.make_async_copy(
                    hidden_ref.at[layer, pl.ds(which * quarter + part * band, band)],
                    hbuf.at[slot, part, pl.ds((which % 2 * 2 + which // 2) * band, band)],
                    load_sem.at[slot, part * 4 + which],
                )
                for which in range(4)
            ]
            for part in range(SPLIT)
        ]
        weight = pltpu.make_async_copy(weight_ref.at[layer], wbuf.at[slot], load_sem.at[slot, SPLIT * 4])
        return rows, weight

    def start_loads(layer):
        rows, weight = loads(layer)
        for part in range(SPLIT):
            for copy in rows[part]:
                copy.start()
            if part == 0:
                weight.start()

    start_loads(0)

    barrier = pltpu.get_barrier_semaphore()
    for peer in (core_peer, x_peer):
        pl.semaphore_signal(barrier, inc=1, device_id={"kdim": peer}, device_id_type=pl.DeviceIdType.MESH)

    def greet(offset, carry):
        pl.semaphore_signal(
            barrier, inc=1, device_id={"head": lax.rem(me + offset, heads)}, device_id_type=pl.DeviceIdType.MESH
        )
        return carry

    lax.fori_loop(1, heads, greet, 0)
    pl.semaphore_wait(barrier, heads + 1)

    def source_of(head):
        found = 0
        for rank in range(heads):
            found = found + jnp.where(group_map_ref[rank] == head, source_block_ref[rank], 0)
        return found

    def remote(source, target, send, recv, peer):
        return pltpu.make_async_remote_copy(
            src_ref=source, dst_ref=target, send_sem=send, recv_sem=recv,
            device_id=peer, device_id_type=pl.DeviceIdType.MESH,
        )

    def core_copy(stage):
        return remote(
            core_out.at[stage], core_in.at[stage], core_send.at[stage], core_recv.at[stage], {"kdim": core_peer}
        )

    def x_copies(stage):
        return (
            remote(x_out.at[stage], x_in.at[stage], x_send.at[stage, 0], x_recv.at[stage, 0], {"kdim": x_peer}),
            remote(
                x_scale_out.at[stage], x_scale_in.at[stage], x_send.at[stage, 1], x_recv.at[stage, 1],
                {"kdim": x_peer},
            ),
        )

    def spread_copies(stage, peer, slot):
        return (
            remote(
                spread_out.at[stage, peer], spread_in[stage].at[slot], p_send.at[stage, peer],
                p_recv.at[stage, slot], {"head": peer},
            ),
            remote(
                own_scale.at[stage], scale_ref.at[stage, slot], s_send.at[stage, peer],
                s_recv.at[stage, slot], {"head": peer},
            ),
        )

    def bound_copy(stage, peer, slot):
        return remote(
            bound_out.at[stage, peer], out_ref.at[stage, slot], b_send.at[stage, peer],
            b_recv.at[stage, slot], {"head": peer},
        )

    def own_scale_copy(stage):
        return pltpu.make_async_copy(own_scale.at[stage], scale_ref.at[stage, me], s_recv.at[stage, me])

    def own_bound_copy(stage):
        return pltpu.make_async_copy(bound_out.at[stage, me], out_ref.at[stage, me], b_recv.at[stage, me])

    width = 256
    tiles = columns // width
    chunks = band // CHUNK

    def product(stage, which_core, target):
        slot, part = (stage // SPLIT) % 2, stage % SPLIT
        row = pl.multiple_of(which_core * 2 * band, 2 * band)

        def body(tile, carry):
            column = pl.multiple_of(tile * width, width)
            both = jnp.dot(
                hbuf[slot, part, pl.ds(row, 2 * band), :], wbuf[slot, :, pl.ds(column, width)],
                preferred_element_type=jnp.float32,
            )
            target[0, :, pl.ds(column, width)] = both[:band]
            target[1, :, pl.ds(column, width)] = both[band:]
            return carry

        lax.fori_loop(0, tiles, body, 0)

    def rows_of(chunk):
        return pl.ds(pl.multiple_of(chunk * CHUNK, CHUNK), CHUNK)

    zero_peak = jnp.zeros((8, 128), jnp.float32)

    def multiply(stage):
        rows, weight = loads(stage // SPLIT)
        for copy in rows[stage % SPLIT]:
            copy.wait()
        if stage % SPLIT == 0:
            weight.wait()
        if stage == 0 and layers > 1:
            start_loads(1)
        product(stage, 1 - core, core_out.at[stage])
        core_copy(stage).start()
        product(stage, core, mine)
        layer = stage // SPLIT
        if stage % SPLIT == SPLIT - 1 and layer + 2 < layers:
            start_loads(layer + 2)
        core_copy(stage).wait_recv()

        def add(chunk, peak):
            rows = rows_of(chunk)
            hold[stage, rows, :] = mine[x, rows, :] + core_in[stage, x, rows, :]
            other = mine[1 - x, rows, :] + core_in[stage, 1 - x, rows, :]
            mine[1 - x, rows, :] = other
            return jnp.maximum(peak, fold_peak(other))

        inverse, scale = quantum(lax.fori_loop(0, chunks, add, zero_peak))
        x_scale_out[stage] = scale
        inverse = spread_tile(inverse, columns)

        def pack(chunk, carry):
            rows = rows_of(chunk)
            x_out[stage, rows, :] = code(mine[1 - x, rows, :], inverse)
            return carry

        lax.fori_loop(0, chunks, pack, 0)
        for copy in x_copies(stage):
            copy.start()

    def reduce(stage):
        for copy in x_copies(stage):
            copy.wait_recv()
        arrived = spread_tile(x_scale_in[stage], columns)

        def add(chunk, peak):
            rows = rows_of(chunk)
            total = hold[stage, rows, :] + decode(x_in[stage, rows, :], arrived)
            hold[stage, rows, :] = total
            return jnp.maximum(peak, fold_peak(total))

        peak = lax.fori_loop(0, chunks, add, zero_peak)
        inverse, scale = quantum(jnp.max(peak, axis=0, keepdims=True))
        own_scale[stage] = scale
        inverse = jnp.concatenate([inverse] * (columns // 128), axis=1)
        per = chunks // heads

        def pack(chunk, carry):
            spread_out[stage, lax.div(chunk, per), rows_of(lax.rem(chunk, per)), :] = code(
                hold[stage, rows_of(chunk), :], inverse
            )
            return carry

        lax.fori_loop(0, chunks, pack, 0)

        def send(offset, carry):
            for copy in spread_copies(stage, lax.rem(me + offset, heads), me):
                copy.start()
            return carry

        lax.fori_loop(1, heads, send, 0)
        own_scale_copy(stage).start()
        spread_in[stage][me] = spread_out[stage, me]

    def forward(stage):
        def arrive(offset, carry):
            peer = lax.rem(me + offset, heads)
            spread_copies(stage, peer, peer)[0].wait_recv()
            return carry

        lax.fori_loop(1, heads, arrive, 0)

        def send(offset, carry):
            peer = lax.rem(me + offset, heads)
            bound_out[stage, peer] = spread_in[stage][source_of(peer)]
            bound_copy(stage, peer, me).start()
            return carry

        lax.fori_loop(1, heads, send, 0)
        bound_out[stage, me] = spread_in[stage][source_of(me)]
        own_bound_copy(stage).start()

    for step in range(stages + 4):
        if step < stages:
            multiply(step)
        if 0 <= step - 1 < stages:
            reduce(step - 1)
        if 0 <= step - 2 < stages:
            forward(step - 2)

    def finish(stage, carry):
        core_copy(stage).wait_send()
        for copy in x_copies(stage):
            copy.wait_send()

        def one(offset, inner):
            peer = lax.rem(me + offset, heads)
            for copy in (
                remote(
                    spread_out.at[stage, peer], out_ref.at[stage, peer], p_send.at[stage, peer],
                    p_recv.at[stage, peer], {"head": peer},
                ),
                remote(
                    own_scale.at[stage], scale_ref.at[stage, peer], s_send.at[stage, peer],
                    s_recv.at[stage, peer], {"head": peer},
                ),
                bound_copy(stage, peer, peer),
            ):
                copy.wait_send()
            spread_scale = remote(
                own_scale.at[stage], scale_ref.at[stage, peer], s_send.at[stage, peer],
                s_recv.at[stage, peer], {"head": peer},
            )
            spread_scale.wait_recv()
            bound_copy(stage, peer, peer).wait_recv()
            return inner

        lax.fori_loop(1, heads, one, 0)
        own_scale_copy(stage).wait()
        own_bound_copy(stage).wait()
        return carry

    lax.fori_loop(0, stages, finish, 0)


def place_kernel(source_block_ref, group_map_ref, q_slot_ref, coded_ref, scale_ref, out_ref):
    me = lax.axis_index("head")
    rank = 0
    for other in range(KV_HEADS):
        rank = rank + jnp.where(group_map_ref[other] == me, other, 0)
    mine = source_block_ref[rank]
    scales = [scale_ref[part, mine] for part in range(SPLIT)]
    for slot in range(GROUP):
        local = 0
        for member in range(GROUP):
            local = local + jnp.where(q_slot_ref[rank * GROUP + member] == slot, member, 0)
        start = pl.multiple_of(local * HEAD_DIM, HEAD_DIM)
        for part in range(SPLIT):
            out_ref[part, :, slot * HEAD_DIM : (slot + 1) * HEAD_DIM] = decode(
                coded_ref[part, :, pl.ds(start, HEAD_DIM)], scales[part]
            )
    for start in range(GROUP * HEAD_DIM, coded_ref.shape[2], HEAD_DIM):
        for part in range(SPLIT):
            out_ref[part, :, start : start + HEAD_DIM] = decode(
                coded_ref[part, :, start : start + HEAD_DIM], scales[part]
            )


def fused(hidden, joined_weight, src_block, group_map, q_slot):
    layers, rows, depth = hidden.shape
    columns = joined_weight.shape[2]
    heads = lax.axis_size("head")
    stages = layers * SPLIT
    band = rows // 4 // SPLIT
    piece = band // heads
    f32, i16 = jnp.float32, jnp.int16
    hbm = pl.BlockSpec(memory_space=pl.ANY)
    dma = pltpu.SemaphoreType.DMA
    coded, scales = pl.pallas_call(
        functools.partial(exchange_kernel, layers, heads, stages, band),
        out_shape=[
            jax.ShapeDtypeStruct((stages, heads, piece, columns), i16),
            jax.ShapeDtypeStruct((stages, heads, 1, 128), f32),
        ],
        in_specs=[pl.BlockSpec(memory_space=pltpu.SMEM)] * 2 + [hbm, hbm],
        out_specs=[hbm, hbm],
        scratch_shapes=[
            pltpu.VMEM((2, SPLIT, 4 * band, depth), hidden.dtype),
            pltpu.VMEM((2, depth, columns), joined_weight.dtype),
            pltpu.VMEM((stages, 2, band, columns), f32),
            pltpu.VMEM((stages, 2, band, columns), f32),
            pltpu.VMEM((2, band, columns), f32),
            pltpu.VMEM((stages, band, columns), f32),
            pltpu.VMEM((stages, band, columns), i16),
            pltpu.VMEM((stages, band, columns), i16),
            pltpu.VMEM((stages, 8, 128), f32),
            pltpu.VMEM((stages, 8, 128), f32),
            pltpu.VMEM((stages, heads, piece, columns), i16),
            pltpu.VMEM((stages, 1, 128), f32),
            pltpu.VMEM((stages, heads, piece, columns), i16),
        ]
        + [pltpu.VMEM((heads, piece, columns), i16) for _ in range(stages)]
        + [dma((2, SPLIT * 4 + 1)), dma((stages,)), dma((stages,)), dma((stages, 2)), dma((stages, 2))]
        + [dma((stages, heads)) for _ in range(6)],
        compiler_params=pltpu.CompilerParams(
            collective_id=0, has_side_effects=True, vmem_limit_bytes=58 * 2**20
        ),
        cost_estimate=pl.CostEstimate(
            flops=2 * layers * rows * depth * columns, transcendentals=0,
            bytes_accessed=2 * layers * depth * (rows + columns),
        ),
    )(src_block, group_map, hidden, joined_weight)
    out = pl.pallas_call(
        place_kernel,
        grid_spec=pltpu.PrefetchScalarGridSpec(
            num_scalar_prefetch=3,
            grid=(layers,),
            in_specs=[
                pl.BlockSpec((SPLIT, band, columns), lambda s, *tables: (s, 0, 0)),
                pl.BlockSpec((SPLIT, heads, 1, 128), lambda s, *tables: (s, 0, 0, 0)),
            ],
            out_specs=pl.BlockSpec((SPLIT, band, columns), lambda s, *tables: (s, 0, 0)),
        ),
        out_shape=jax.ShapeDtypeStruct((stages, band, columns), f32),
    )(src_block, group_map, q_slot, coded.reshape(stages, band, columns), scales)
    return out.reshape(layers, rows // 4, columns)


def on_device(hidden, joined_weight, src_block, group_map, q_slot):
    head_count = lax.axis_size("head")
    per_group = head_count // KV_HEADS
    low_bits = per_group.bit_length() - 1
    sort_bits = KV_HEADS.bit_length() - 1
    slot_count = Q_HEADS // head_count
    head_index = lax.axis_index("head")
    position = head_index // per_group
    quarter = head_index % per_group
    rank_ids = jnp.arange(KV_HEADS, dtype=jnp.int32)
    rank_at = jnp.sum(rank_ids[None, :] * (src_block[None, :] == rank_ids[:, None]), axis=1)
    start_keys = lookup(group_map, rank_at)
    rank_here = jnp.sum(rank_ids * (group_map == position))
    group_slots = lax.dynamic_slice_in_dim(q_slot, rank_here * GROUP, GROUP)
    heads_fit = head_count == KV_HEADS and joined_weight.shape[2] == (GROUP + 2) * HEAD_DIM
    if heads_fit and lax.axis_size("kdim") == 4 and hidden.shape[1] % (4 * SPLIT * CHUNK * head_count) == 0:
        return fused(hidden, joined_weight, src_block, group_map, q_slot)
    partial_value = jnp.einsum(
        "lrd,ldc->lrc", hidden, joined_weight, preferred_element_type=jnp.float32
    )
    summed = lax.psum_scatter(partial_value, "kdim", scatter_dimension=1, tiled=True)
    return regroup(
        summed,
        start_keys,
        position,
        quarter,
        head_index,
        group_slots,
        slot_count,
        low_bits,
        sort_bits,
        lambda piece, which_bit: from_partner(piece, "head", which_bit),
        lambda piece, which_bit: from_partner(piece, "head", which_bit),
    )


def solution(mesh):
    return jax.shard_map(
        on_device,
        mesh=mesh,
        in_specs=(P(None, None, "kdim"), P(None, "kdim", "head"), P(), P(), P()),
        out_specs=P(None, "kdim", "head"),
        check_vma=False,
    )
```

```python
import jax
import jax.numpy as jnp
from jax import lax
import functools
from jax.experimental import pallas as pl
from jax.experimental.pallas import tpu as pltpu
from jax.sharding import PartitionSpec as P

HEAD_DIM = 128
Q_HEADS = 64
KV_HEADS = 8
GROUP = 8


def from_partner(block, axis, stride):
    count = lax.axis_size(axis)
    route = []
    for low in range(count):
        high = low | 1 << stride
        if high != low and high < count:
            route += [(low, high), (high, low)]
    return lax.ppermute(block, axis, route)


def lookup(table, where_at):
    entries = jnp.arange(table.shape[0], dtype=jnp.int32)
    return jnp.sum(table[None, :] * (entries[None, :] == where_at[:, None]), axis=1)


def regroup(
    payload,
    start_keys,
    position,
    quarter,
    head_index,
    group_slots,
    slot_count,
    low_bits,
    sort_bits,
    pair_swap,
    part_swap,
):
    places = jnp.arange(KV_HEADS, dtype=jnp.int32)
    key_list = start_keys
    for level in range(1, sort_bits + 1):
        for stride in reversed(range(level)):
            partner = pair_swap(payload, low_bits + stride)
            partner_places = jnp.bitwise_xor(places, 1 << stride)
            partner_keys = lookup(key_list, partner_places)
            upper_half = jnp.bitwise_and(jnp.right_shift(places, stride), 1) == 1
            ascending = jnp.bitwise_and(jnp.right_shift(places, level), 1) == 0
            smaller = key_list < partner_keys
            keep_own = (jnp.logical_not(upper_half) == smaller) == ascending
            keep_mine = jnp.any(jnp.logical_and(keep_own, places == position))
            payload = jnp.where(keep_mine, payload, partner)
            key_list = jnp.where(keep_own, key_list, partner_keys)
    for which_bit in range(low_bits):
        partner = part_swap(payload, which_bit)
        upper_side = jnp.bitwise_and(jnp.right_shift(head_index, which_bit), 1) == 1
        payload = jnp.where(
            upper_side,
            jnp.concatenate([partner, payload], axis=2),
            jnp.concatenate([payload, partner], axis=2),
        )
    pieces = []
    for offset_slot in range(slot_count):
        wanted = quarter * slot_count + offset_slot
        local_head = jnp.sum(jnp.arange(GROUP, dtype=jnp.int32) * (group_slots == wanted))
        pieces.append(lax.dynamic_slice_in_dim(payload, local_head * HEAD_DIM, HEAD_DIM, axis=2))
    pieces.append(payload[:, :, GROUP * HEAD_DIM :])
    return jnp.concatenate(pieces, axis=2)


SPLIT = 2
TOP = 32767.0
TINY = 1e-30
CHUNK = 16


def quantum(peak):
    peak = jnp.maximum(peak, TINY)
    return TOP / peak, peak * (1.0 / TOP)


def spread_tile(tile, columns):
    return jnp.concatenate([jnp.concatenate([tile] * (CHUNK // 8), axis=0)] * (columns // 128), axis=1)


def fold_peak(value):
    value = jnp.abs(value)
    peak = value[:, :128]
    for start in range(128, value.shape[1], 128):
        peak = jnp.maximum(peak, value[:, start : start + 128])
    return jnp.maximum(peak[:8], peak[8:])


def code(value, inverse):
    return jnp.round(value * inverse).astype(jnp.int32).astype(jnp.int16)


def decode(coded, scale):
    return coded.astype(jnp.int32).astype(jnp.float32) * scale


def exchange_kernel(
    layers, heads, stages, band, source_block_ref, group_map_ref, hidden_ref, weight_ref, out_ref, scale_ref,
    hbuf, wbuf, core_out, core_in, mine, hold, x_out, x_in, x_scale_out, x_scale_in,
    spread_out, own_scale, bound_out, *rest,
):
    spread_in = rest[:stages]
    load_sem, core_send, core_recv, x_send, x_recv, p_send, p_recv, s_send, s_recv, b_send, b_recv = rest[stages:]
    columns = weight_ref.shape[2]
    quarter = hidden_ref.shape[1] // 4
    me = lax.axis_index("head")
    k = lax.axis_index("kdim")
    core, x = lax.rem(k, 2), lax.div(k, 2)
    core_peer = x * 2 + 1 - core
    x_peer = (1 - x) * 2 + core

    def loads(layer):
        slot = layer % 2
        rows = [
            [
                pltpu.make_async_copy(
                    hidden_ref.at[layer, pl.ds(which * quarter + part * band, band)],
                    hbuf.at[slot, part, pl.ds((which % 2 * 2 + which // 2) * band, band)],
                    load_sem.at[slot, part * 4 + which],
                )
                for which in range(4)
            ]
            for part in range(SPLIT)
        ]
        weight = pltpu.make_async_copy(weight_ref.at[layer], wbuf.at[slot], load_sem.at[slot, SPLIT * 4])
        return rows, weight

    def start_loads(layer):
        rows, weight = loads(layer)
        for part in range(SPLIT):
            for copy in rows[part]:
                copy.start()
            if part == 0:
                weight.start()

    start_loads(0)

    barrier = pltpu.get_barrier_semaphore()
    for peer in (core_peer, x_peer):
        pl.semaphore_signal(barrier, inc=1, device_id={"kdim": peer}, device_id_type=pl.DeviceIdType.MESH)

    def greet(offset, carry):
        pl.semaphore_signal(
            barrier, inc=1, device_id={"head": lax.rem(me + offset, heads)}, device_id_type=pl.DeviceIdType.MESH
        )
        return carry

    lax.fori_loop(1, heads, greet, 0)
    pl.semaphore_wait(barrier, heads + 1)

    def far_first(turn):
        return lax.rem(me + heads // 2 + lax.div(turn, 2) * (1 - 2 * lax.rem(turn, 2)), heads)

    def source_of(head):
        found = 0
        for rank in range(heads):
            found = found + jnp.where(group_map_ref[rank] == head, source_block_ref[rank], 0)
        return found

    def remote(source, target, send, recv, peer):
        return pltpu.make_async_remote_copy(
            src_ref=source, dst_ref=target, send_sem=send, recv_sem=recv,
            device_id=peer, device_id_type=pl.DeviceIdType.MESH,
        )

    def core_copy(stage):
        return remote(
            core_out.at[stage], core_in.at[stage], core_send.at[stage], core_recv.at[stage], {"kdim": core_peer}
        )

    def x_copies(stage):
        return (
            remote(x_out.at[stage], x_in.at[stage], x_send.at[stage, 0], x_recv.at[stage, 0], {"kdim": x_peer}),
            remote(
                x_scale_out.at[stage], x_scale_in.at[stage], x_send.at[stage, 1], x_recv.at[stage, 1],
                {"kdim": x_peer},
            ),
        )

    def spread_copies(stage, peer, slot):
        return (
            remote(
                spread_out.at[stage, peer], spread_in[stage].at[slot], p_send.at[stage, peer],
                p_recv.at[stage, slot], {"head": peer},
            ),
            remote(
                own_scale.at[stage], scale_ref.at[stage, slot], s_send.at[stage, peer],
                s_recv.at[stage, slot], {"head": peer},
            ),
        )

    def bound_copy(stage, peer, slot):
        return remote(
            bound_out.at[stage, peer], out_ref.at[stage, slot], b_send.at[stage, peer],
            b_recv.at[stage, slot], {"head": peer},
        )

    def own_scale_copy(stage):
        return pltpu.make_async_copy(own_scale.at[stage], scale_ref.at[stage, me], s_recv.at[stage, me])

    def own_bound_copy(stage):
        return pltpu.make_async_copy(bound_out.at[stage, me], out_ref.at[stage, me], b_recv.at[stage, me])

    width = 256
    tiles = columns // width
    chunks = band // CHUNK

    def product(stage, which_core, target):
        slot, part = (stage // SPLIT) % 2, stage % SPLIT
        row = pl.multiple_of(which_core * 2 * band, 2 * band)

        def body(tile, carry):
            column = pl.multiple_of(tile * width, width)
            both = jnp.dot(
                hbuf[slot, part, pl.ds(row, 2 * band), :], wbuf[slot, :, pl.ds(column, width)],
                preferred_element_type=jnp.float32,
            )
            target[0, :, pl.ds(column, width)] = both[:band]
            target[1, :, pl.ds(column, width)] = both[band:]
            return carry

        lax.fori_loop(0, tiles, body, 0)

    def rows_of(chunk):
        return pl.ds(pl.multiple_of(chunk * CHUNK, CHUNK), CHUNK)

    zero_peak = jnp.zeros((8, 128), jnp.float32)

    def multiply(stage):
        rows, weight = loads(stage // SPLIT)
        for copy in rows[stage % SPLIT]:
            copy.wait()
        if stage % SPLIT == 0:
            weight.wait()
        if stage == 0 and layers > 1:
            start_loads(1)
        product(stage, 1 - core, core_out.at[stage])
        core_copy(stage).start()
        product(stage, core, mine)
        layer = stage // SPLIT
        if stage % SPLIT == SPLIT - 1 and layer + 2 < layers:
            start_loads(layer + 2)
        core_copy(stage).wait_recv()

        def add(chunk, peak):
            rows = rows_of(chunk)
            hold[stage, rows, :] = mine[x, rows, :] + core_in[stage, x, rows, :]
            other = mine[1 - x, rows, :] + core_in[stage, 1 - x, rows, :]
            mine[1 - x, rows, :] = other
            return jnp.maximum(peak, fold_peak(other))

        inverse, scale = quantum(lax.fori_loop(0, chunks, add, zero_peak))
        x_scale_out[stage] = scale
        inverse = spread_tile(inverse, columns)

        def pack(chunk, carry):
            rows = rows_of(chunk)
            x_out[stage, rows, :] = code(mine[1 - x, rows, :], inverse)
            return carry

        lax.fori_loop(0, chunks, pack, 0)
        for copy in x_copies(stage):
            copy.start()

    def reduce(stage):
        for copy in x_copies(stage):
            copy.wait_recv()
        arrived = spread_tile(x_scale_in[stage], columns)

        def add(chunk, peak):
            rows = rows_of(chunk)
            total = hold[stage, rows, :] + decode(x_in[stage, rows, :], arrived)
            hold[stage, rows, :] = total
            return jnp.maximum(peak, fold_peak(total))

        peak = lax.fori_loop(0, chunks, add, zero_peak)
        inverse, scale = quantum(jnp.max(peak, axis=0, keepdims=True))
        own_scale[stage] = scale
        inverse = jnp.concatenate([inverse] * (columns // 128), axis=1)
        per = chunks // heads

        def pack(chunk, carry):
            spread_out[stage, lax.div(chunk, per), rows_of(lax.rem(chunk, per)), :] = code(
                hold[stage, rows_of(chunk), :], inverse
            )
            return carry

        lax.fori_loop(0, chunks, pack, 0)

        def send(offset, carry):
            for copy in spread_copies(stage, far_first(offset), me):
                copy.start()
            return carry

        lax.fori_loop(1, heads, send, 0)
        own_scale_copy(stage).start()
        spread_in[stage][me] = spread_out[stage, me]

    def forward(stage):
        def arrive(offset, carry):
            peer = lax.rem(me + offset, heads)
            spread_copies(stage, peer, peer)[0].wait_recv()
            return carry

        lax.fori_loop(1, heads, arrive, 0)

        def send(offset, carry):
            peer = far_first(offset)
            bound_out[stage, peer] = spread_in[stage][source_of(peer)]
            bound_copy(stage, peer, me).start()
            return carry

        lax.fori_loop(1, heads, send, 0)
        bound_out[stage, me] = spread_in[stage][source_of(me)]
        own_bound_copy(stage).start()

    for step in range(stages + 4):
        if step < stages:
            multiply(step)
        if 0 <= step - 1 < stages:
            reduce(step - 1)
        if 0 <= step - 3 < stages:
            forward(step - 3)

    def finish(stage, carry):
        core_copy(stage).wait_send()
        for copy in x_copies(stage):
            copy.wait_send()

        def one(offset, inner):
            peer = lax.rem(me + offset, heads)
            for copy in (
                remote(
                    spread_out.at[stage, peer], out_ref.at[stage, peer], p_send.at[stage, peer],
                    p_recv.at[stage, peer], {"head": peer},
                ),
                remote(
                    own_scale.at[stage], scale_ref.at[stage, peer], s_send.at[stage, peer],
                    s_recv.at[stage, peer], {"head": peer},
                ),
                bound_copy(stage, peer, peer),
            ):
                copy.wait_send()
            spread_scale = remote(
                own_scale.at[stage], scale_ref.at[stage, peer], s_send.at[stage, peer],
                s_recv.at[stage, peer], {"head": peer},
            )
            spread_scale.wait_recv()
            bound_copy(stage, peer, peer).wait_recv()
            return inner

        lax.fori_loop(1, heads, one, 0)
        own_scale_copy(stage).wait()
        own_bound_copy(stage).wait()
        return carry

    lax.fori_loop(0, stages, finish, 0)


def place_kernel(source_block_ref, group_map_ref, q_slot_ref, coded_ref, scale_ref, out_ref):
    me = lax.axis_index("head")
    rank = 0
    for other in range(KV_HEADS):
        rank = rank + jnp.where(group_map_ref[other] == me, other, 0)
    mine = source_block_ref[rank]
    scales = [scale_ref[part, mine] for part in range(SPLIT)]
    for slot in range(GROUP):
        local = 0
        for member in range(GROUP):
            local = local + jnp.where(q_slot_ref[rank * GROUP + member] == slot, member, 0)
        start = pl.multiple_of(local * HEAD_DIM, HEAD_DIM)
        for part in range(SPLIT):
            out_ref[part, :, slot * HEAD_DIM : (slot + 1) * HEAD_DIM] = decode(
                coded_ref[part, :, pl.ds(start, HEAD_DIM)], scales[part]
            )
    for start in range(GROUP * HEAD_DIM, coded_ref.shape[2], HEAD_DIM):
        for part in range(SPLIT):
            out_ref[part, :, start : start + HEAD_DIM] = decode(
                coded_ref[part, :, start : start + HEAD_DIM], scales[part]
            )


def fused(hidden, joined_weight, src_block, group_map, q_slot):
    layers, rows, depth = hidden.shape
    columns = joined_weight.shape[2]
    heads = lax.axis_size("head")
    stages = layers * SPLIT
    band = rows // 4 // SPLIT
    piece = band // heads
    f32, i16 = jnp.float32, jnp.int16
    hbm = pl.BlockSpec(memory_space=pl.ANY)
    dma = pltpu.SemaphoreType.DMA
    coded, scales = pl.pallas_call(
        functools.partial(exchange_kernel, layers, heads, stages, band),
        out_shape=[
            jax.ShapeDtypeStruct((stages, heads, piece, columns), i16),
            jax.ShapeDtypeStruct((stages, heads, 1, 128), f32),
        ],
        in_specs=[pl.BlockSpec(memory_space=pltpu.SMEM)] * 2 + [hbm, hbm],
        out_specs=[hbm, hbm],
        scratch_shapes=[
            pltpu.VMEM((2, SPLIT, 4 * band, depth), hidden.dtype),
            pltpu.VMEM((2, depth, columns), joined_weight.dtype),
            pltpu.VMEM((stages, 2, band, columns), f32),
            pltpu.VMEM((stages, 2, band, columns), f32),
            pltpu.VMEM((2, band, columns), f32),
            pltpu.VMEM((stages, band, columns), f32),
            pltpu.VMEM((stages, band, columns), i16),
            pltpu.VMEM((stages, band, columns), i16),
            pltpu.VMEM((stages, 8, 128), f32),
            pltpu.VMEM((stages, 8, 128), f32),
            pltpu.VMEM((stages, heads, piece, columns), i16),
            pltpu.VMEM((stages, 1, 128), f32),
            pltpu.VMEM((stages, heads, piece, columns), i16),
        ]
        + [pltpu.VMEM((heads, piece, columns), i16) for _ in range(stages)]
        + [dma((2, SPLIT * 4 + 1)), dma((stages,)), dma((stages,)), dma((stages, 2)), dma((stages, 2))]
        + [dma((stages, heads)) for _ in range(6)],
        compiler_params=pltpu.CompilerParams(
            collective_id=0, has_side_effects=True, vmem_limit_bytes=58 * 2**20
        ),
        cost_estimate=pl.CostEstimate(
            flops=2 * layers * rows * depth * columns, transcendentals=0,
            bytes_accessed=2 * layers * depth * (rows + columns),
        ),
    )(src_block, group_map, hidden, joined_weight)
    out = pl.pallas_call(
        place_kernel,
        grid_spec=pltpu.PrefetchScalarGridSpec(
            num_scalar_prefetch=3,
            grid=(layers,),
            in_specs=[
                pl.BlockSpec((SPLIT, band, columns), lambda s, *tables: (s, 0, 0)),
                pl.BlockSpec((SPLIT, heads, 1, 128), lambda s, *tables: (s, 0, 0, 0)),
            ],
            out_specs=pl.BlockSpec((SPLIT, band, columns), lambda s, *tables: (s, 0, 0)),
        ),
        out_shape=jax.ShapeDtypeStruct((stages, band, columns), f32),
    )(src_block, group_map, q_slot, coded.reshape(stages, band, columns), scales)
    return out.reshape(layers, rows // 4, columns)


def on_device(hidden, joined_weight, src_block, group_map, q_slot):
    head_count = lax.axis_size("head")
    per_group = head_count // KV_HEADS
    low_bits = per_group.bit_length() - 1
    sort_bits = KV_HEADS.bit_length() - 1
    slot_count = Q_HEADS // head_count
    head_index = lax.axis_index("head")
    position = head_index // per_group
    quarter = head_index % per_group
    rank_ids = jnp.arange(KV_HEADS, dtype=jnp.int32)
    rank_at = jnp.sum(rank_ids[None, :] * (src_block[None, :] == rank_ids[:, None]), axis=1)
    start_keys = lookup(group_map, rank_at)
    rank_here = jnp.sum(rank_ids * (group_map == position))
    group_slots = lax.dynamic_slice_in_dim(q_slot, rank_here * GROUP, GROUP)
    heads_fit = head_count == KV_HEADS and joined_weight.shape[2] == (GROUP + 2) * HEAD_DIM
    if heads_fit and lax.axis_size("kdim") == 4 and hidden.shape[1] % (4 * SPLIT * CHUNK * head_count) == 0:
        return fused(hidden, joined_weight, src_block, group_map, q_slot)
    partial_value = jnp.einsum(
        "lrd,ldc->lrc", hidden, joined_weight, preferred_element_type=jnp.float32
    )
    summed = lax.psum_scatter(partial_value, "kdim", scatter_dimension=1, tiled=True)
    return regroup(
        summed,
        start_keys,
        position,
        quarter,
        head_index,
        group_slots,
        slot_count,
        low_bits,
        sort_bits,
        lambda piece, which_bit: from_partner(piece, "head", which_bit),
        lambda piece, which_bit: from_partner(piece, "head", which_bit),
    )


def solution(mesh):
    return jax.shard_map(
        on_device,
        mesh=mesh,
        in_specs=(P(None, None, "kdim"), P(None, "kdim", "head"), P(), P(), P()),
        out_specs=P(None, "kdim", "head"),
        check_vma=False,
    )
```
